32 devices in a mesh: depth: 4 (over y, core), lat: 8 (over z, x).
Axes of the slice: x: 2, y: 2, z: 4, core: 2. Of those that a mesh axis runs over, the one named last changes fastest.
Arguments:
- slices: float32 [12, 2, 256, 2048], P('depth', None, None, 'lat'), may hold values from -1.23 to 1.23, as said below
- section_counts: int32 [4], P('depth'), may hold values from 1 to 3, as said below
- scan_rows: int32 [64], P('lat'), may hold values from 0 to 128, as said below
- scan_columns: int32 [64], P('lat'), may hold values from 0 to 256, as said below
- tick_order: int32 [8, 8], P('lat'), may hold values from 0 to 7, each once within a row
- measured: float32 [64, 128, 128], P('lat'), may hold values from 0.2 to 2
- illumination: float32 [2, 128, 128], replicated, may hold values from -4.2 to 4.2
Outputs:
- slice_grad: float32 [12, 2, 256, 2048], P('depth', None, None, 'lat')
- position_loss: float32 [8, 8], P('lat')
The draws below stay inside these ranges and needn't reach their ends.
Inputs may be any that keep to these rules, and one draw needn't show every extreme that they name: `slices`: the real and imaginary parts of transmission values of magnitude near one. `section_counts`: some section uses all 3 slots and some other section uses one. `scan_rows`: both ends are reached in every draw. `scan_columns`: a window may reach up to 128 columns into the next tile, the last tile continuing into the first; both ends are reached in every draw. `tick_order`: each row lists the tile's 8 positions once.
All inputs are finite; a program needn't handle non-finite values.
Results may differ from the reference program's by a relative error of at most 0.0003.
Values sent between devices are 32-bit elements; how exact they have to be, the bound alone decides.
A program may use at most 128 MiB of HBM per device.

```python
import math
import jax
import jax.numpy as jnp
from jax import lax

W = 128
TILE = 256
MAXS = 3
POS = 8
SLOTS = 12
POSITIONS = 64
N_DEPTH = 4
N_LAT = 8


def draw_slices(key, part):
    first, second = jax.random.split(key)
    shape = (SLOTS, TILE, TILE * N_LAT)
    amplitude = jnp.exp(jax.random.uniform(first, shape, jnp.float32, -0.2, 0.2))
    phase = jax.random.uniform(second, shape, jnp.float32, -jnp.pi, jnp.pi)
    return jnp.stack([amplitude * jnp.cos(phase), amplitude * jnp.sin(phase)], axis=1)


def draw_section_counts(key, part):
    first, second, third = jax.random.split(jax.random.fold_in(key, 11), 3)
    values = jax.random.randint(first, (N_DEPTH,), 1, MAXS + 1)
    place = jax.random.randint(second, (), 0, N_DEPTH)
    other = (place + 1 + jax.random.randint(third, (), 0, N_DEPTH - 1)) % N_DEPTH
    return values.at[other].set(1).at[place].set(MAXS)


def ends_draw(key, top):
    first, second, third = jax.random.split(key, 3)
    values = jax.random.randint(first, (POS * N_LAT,), 0, top + 1)
    place = jax.random.randint(second, (), 0, POS * N_LAT)
    other = (place + 1 + jax.random.randint(third, (), 0, POS * N_LAT - 1)) % (POS * N_LAT)
    return values.at[other].set(0).at[place].set(top)


def draw_scan_rows(key, part):
    return ends_draw(jax.random.fold_in(key, 23), TILE - W)


def draw_scan_columns(key, part):
    return ends_draw(jax.random.fold_in(key, 37), TILE)


def levels(stream_key, dims, cuts, low, largest):
    level, own = 1.0, jax.random.fold_in(stream_key, 6)
    for axis_at, shards_of in cuts:
        steps = jnp.exp(jax.random.uniform(jax.random.fold_in(own, axis_at), (shards_of,), jnp.float32, low / len(cuts), largest / len(cuts)))
        level = level * jnp.repeat(steps, dims[axis_at] // shards_of).reshape([-1 if axis == axis_at else 1 for axis in range(len(dims))])
    return level


def scatter_about(key, dims, scale, limit, kind=jnp.bfloat16):
    return jnp.clip(scale * jax.random.normal(key, dims, jnp.float32), -limit, limit).astype(kind)


def setup_inputs(seed: int = 0) -> dict:
    key_list = jax.random.split(jax.random.key(seed), 8)
    return {
        "slices": draw_slices(jax.random.fold_in(key_list[7], 71), 0),
        "section_counts": draw_section_counts(jax.random.fold_in(key_list[7], 71), 0),
        "scan_rows": draw_scan_rows(jax.random.fold_in(key_list[7], 71), 0),
        "scan_columns": draw_scan_columns(jax.random.fold_in(key_list[7], 71), 0),
        "tick_order": jax.vmap(lambda own: jax.random.permutation(own, POS))(jax.random.split(key_list[4], N_LAT)).reshape((N_LAT, POS)).astype(jnp.int32),
        "measured": jnp.clip(0.2 + 1.8 * jax.random.uniform(key_list[5], (POSITIONS, W, W), jnp.float32) ** levels(key_list[5], (POSITIONS, W, W), ((0, 8),), -0.2, 0.2), 0.2, 2.0),
        "illumination": scatter_about(key_list[6], (2, W, W), 0.7, 4.2, jnp.float32),
    }


fresnel = 12.0
highest = lax.Precision.HIGHEST

def dft_blocks(width, sign):
    index = jnp.arange(width, dtype=jnp.int32)
    product = index[:, None] * index[None, :] % width
    angle = 2.0 * math.pi / width * product.astype(jnp.float32)
    scale = 1.0 / math.sqrt(width)
    cosine = jnp.cos(angle) * scale
    sine = sign * jnp.sin(angle) * scale
    return jnp.stack([jnp.stack([cosine, sine]), jnp.stack([-sine, cosine])])

def make_tables(width):
    index = jnp.arange(width, dtype=jnp.int32)
    frequency = ((index + width // 2) % width - width // 2).astype(jnp.float32) / width
    phase = -fresnel * (frequency[:, None] * frequency[:, None] + frequency[None, :] * frequency[None, :])
    return (dft_blocks(width, -1.0), dft_blocks(width, 1.0), jnp.cos(phase), jnp.sin(phase))

def transform(fields, blocks):
    half = jnp.einsum('bcyx,cdxk->bdyk', fields, blocks, precision=highest)
    return jnp.einsum('cdky,bcyx->bdkx', blocks, half, precision=highest)

def complex_product(first, second, conjugate):
    sign = -1.0 if conjugate else 1.0
    first_real = first[:, 0]
    first_imag = sign * first[:, 1]
    real_part = first_real * second[:, 0] - first_imag * second[:, 1]
    imag_part = first_real * second[:, 1] + first_imag * second[:, 0]
    return jnp.stack([real_part, imag_part], axis=1)

def propagate(fields, tables, adjoint):
    forward_blocks, inverse_blocks, kernel_cos, kernel_sin = tables
    spectrum = transform(fields, forward_blocks)
    kernel_imag = -kernel_sin if adjoint else kernel_sin
    real_part = spectrum[:, 0] * kernel_cos - spectrum[:, 1] * kernel_imag
    imag_part = spectrum[:, 0] * kernel_imag + spectrum[:, 1] * kernel_cos
    return transform(jnp.stack([real_part, imag_part], axis=1), inverse_blocks)

def forward_loss(windows, active, start_wave, target, tables):

    def one_slice(fields, inputs):
        window, flag = inputs

        def advance(current):
            return propagate(complex_product(current, window[None], False), tables, False)

        def keep(current):
            return current
        return (lax.cond(flag, advance, keep, fields), None)
    fields, _ = lax.scan(one_slice, start_wave[None], (windows, active))
    spectrum = transform(fields, tables[0])
    misfit = spectrum[0, 0] * spectrum[0, 0] + spectrum[0, 1] * spectrum[0, 1] - target
    return (jnp.sum(misfit * misfit), jnp.mean(misfit * misfit))

def reference(slices, section_counts, scan_rows, scan_columns, tick_order, measured, illumination):
    width = illumination.shape[-1]
    tables = make_tables(width)
    slot_index = jnp.arange(MAXS, dtype=jnp.int32)
    active = (slot_index[None, :] < section_counts[:, None]).reshape(-1)
    zero = jnp.zeros((), jnp.int32)

    def one_tile(carry, tile):
        own = lax.dynamic_slice_in_dim(slices, (tile * TILE).astype(jnp.int32), TILE, 3)
        after = lax.dynamic_slice_in_dim(slices, ((tile + 1) % N_LAT * TILE).astype(jnp.int32), width, 3)
        extended = jnp.concatenate([own, after], axis=3)

        def one_position(gradient, local):
            index = tile * POS + local
            corner = (zero, zero, scan_rows[index].astype(jnp.int32), scan_columns[index].astype(jnp.int32))
            windows = lax.dynamic_slice(extended, corner, (SLOTS, 2, width, width))

            def loss_only(cut):
                return forward_loss(cut, active, illumination, measured[index], tables)
            total, pull, mean = jax.vjp(loss_only, windows, has_aux=True)
            pulled, = pull(jnp.ones_like(total))
            old = lax.dynamic_slice(gradient, corner, (SLOTS, 2, width, width))
            gradient = lax.dynamic_update_slice(gradient, old + pulled, corner)
            return (gradient, mean)
        start = jnp.zeros((SLOTS, 2, TILE, TILE + width), jnp.float32)
        gradient, means = lax.scan(one_position, start, jnp.arange(POS, dtype=jnp.int32))
        ordered = means[tick_order[tile]]
        return (carry, (gradient[..., :TILE], gradient[..., TILE:], ordered))
    _, (main, rims, ordered) = lax.scan(one_tile, jnp.zeros((), jnp.float32), jnp.arange(N_LAT, dtype=jnp.int32))
    main = main.at[..., :width].add(jnp.roll(rims, 1, axis=0))
    slice_grad = jnp.transpose(main, (1, 2, 3, 0, 4)).reshape(SLOTS, 2, TILE, N_LAT * TILE)
    return (slice_grad, ordered)
```

```python
import functools
import math

import jax
import jax.numpy as jnp
import ml_dtypes
import numpy as np
from jax import lax
from jax.experimental import pallas as pl
from jax.experimental.pallas import tpu as pltpu
from jax.sharding import PartitionSpec as P

fresnel = 12.0


def split_table(matrix):
    coarse = matrix.astype(ml_dtypes.bfloat16)
    fine = (matrix - coarse.astype(np.float64)).astype(ml_dtypes.bfloat16)
    return np.stack([coarse, fine])


def make_tables(width):
    index = np.arange(width)
    angle = 2.0 * math.pi / width * (index[:, None] * index[None, :] % width)
    dft = np.exp(-1j * angle) / math.sqrt(width)
    frequency = ((index + width // 2) % width - width // 2) / width
    spread = np.conj(dft) @ (np.exp(-1j * fresnel * frequency**2)[:, None] * dft)
    tables = []
    for matrix in (spread, dft):
        right = np.block([[matrix.real, matrix.imag], [-matrix.imag, matrix.real]])
        left = np.block([[matrix.real, -matrix.imag], [matrix.imag, matrix.real]])
        tables.append(np.stack([split_table(right), split_table(left)]))
    return np.stack(tables)


def halves(value):
    coarse = value.astype(jnp.bfloat16)
    fine = (value - coarse.astype(jnp.float32)).astype(jnp.bfloat16)
    return coarse, fine


def both_sides(parts, tables, which, adjoint):
    width = parts[0].shape[0]
    first, second = (1, 0) if adjoint else (0, 1)
    coarse, fine = halves(jnp.concatenate(parts, axis=0))
    high, low = tables[which, first, 0], tables[which, first, 1]
    half = jnp.dot(
        jnp.concatenate([coarse, fine, coarse], axis=1),
        jnp.concatenate([high, high, low], axis=0),
        preferred_element_type=jnp.float32,
    )
    rows = [half[p * width : (p + 1) * width] for p in range(len(parts))]
    turned = jnp.concatenate(
        [
            jnp.concatenate([r[:, :width] for r in rows], axis=1),
            jnp.concatenate([r[:, width:] for r in rows], axis=1),
        ],
        axis=0,
    )
    coarse, fine = halves(turned)
    high, low = tables[which, second, 0], tables[which, second, 1]
    full = jnp.dot(
        jnp.concatenate([high, high, low], axis=1),
        jnp.concatenate([coarse, fine, coarse], axis=0),
        preferred_element_type=jnp.float32,
    )
    return [
        (full[:width, p * width : (p + 1) * width], full[width:, p * width : (p + 1) * width])
        for p in range(len(parts))
    ]


def stage_kernel(kind, stage, cfg, *refs):
    group, slots, width, tile, share = cfg
    blocks = tile // width
    refs = list(refs)
    meta, tables_hbm, entering_hbm = refs[:3]
    mains, rims = refs[3 : 3 + group], refs[3 + group : 3 + 2 * group]
    refs = refs[3 + 2 * group :]
    if kind == "T":
        measured_hbm, out_hbm, loss_ref = refs[0], refs[1], refs[2 + 2 * group]
        grads = refs[2 : 2 + 2 * group]
        refs = refs[3 + 2 * group :]
    elif kind == "F":
        out_hbm, inner_hbm = refs[0], refs[1]
        refs = refs[2:]
    else:
        inner_hbm = refs[0]
        out_hbm = refs[1 + 2 * group]
        grads = refs[2 + 2 * group : 2 + 4 * group]
        refs = refs[2 + 4 * group :]
    specimen, store, inner, current, tables, wanted, sems = refs

    @pl.when(meta[0] == stage)
    def _():
        core = meta[1]
        copies = []

        def bring(source, target):
            copy = pltpu.make_async_copy(source, target, sems.at[len(copies)])
            copy.start()
            copies.append(copy)

        bring(tables_hbm, tables)
        for j in range(group):
            section = core if j == 0 else 1 - core
            place = pl.ds(section * slots, slots)
            for b in range(blocks):
                bring(mains[j].at[:, :, :, pl.ds(b * width, width)], specimen.at[place, :, b])
            bring(rims[j], specimen.at[place, :, blocks])
        if kind == "B":
            bring(entering_hbm, current)
            bring(inner_hbm, inner)
        else:
            bring(entering_hbm, inner.at[0])
        if kind == "T":
            bring(measured_hbm.at[pl.ds(core * share, share)], wanted)
        if kind != "F":
            for slot in range(group * slots):
                store[slot] = jnp.zeros(store.shape[1:], jnp.float32)
        for copy in copies:
            copy.wait()

        count = meta[2]
        total = meta[2] + meta[3] if group == 2 else meta[2]
        lane = lax.broadcasted_iota(jnp.int32, (width, width), 1)

        def place_of(step):
            later = step >= count
            return jnp.where(later, slots + step - count, step)

        def corner(p):
            row, column = meta[4 + p], meta[4 + share + p]
            block = jnp.minimum(column // width, blocks - 1)
            return row, block, column - block * width

        def window(slot, p):
            row, block, shift = corner(p)
            back = lax.rem(width - shift, width)
            found = []
            for c in range(2):
                here = specimen[slot, c, block, pl.ds(row, width), :]
                after = specimen[slot, c, block + 1, pl.ds(row, width), :]
                found.append(pltpu.roll(jnp.where(lane >= shift, here, after), back, 1))
            return found

        def deposit(slot, p, pull):
            row, block, shift = corner(p)
            turn = lax.rem(shift, width)
            for c in range(2):
                turned = pltpu.roll(pull[c], turn, 1)
                here = jnp.where(lane >= shift, turned, 0.0)
                store[slot, c, block, pl.ds(row, width), :] += here
                store[slot, c, block + 1, pl.ds(row, width), :] += turned - here

        def which(step):
            return jnp.where(step == total - 1, 1, 0) if kind == "T" else 0

        def forward(step, carry):
            slot = place_of(step)
            parts = []
            for p in range(share):
                real, imag = window(slot, p)
                value = inner[step, p]
                first, second = value[:, :width], value[:, width:]
                parts.append(
                    jnp.concatenate(
                        [first * real - second * imag, first * imag + second * real], axis=1
                    )
                )
            results = both_sides(parts, tables, which(step), False)
            for p in range(share):
                inner[step + 1, p] = jnp.concatenate(results[p], axis=1)
            return carry

        def backward(back_step, carry):
            step = total - 1 - back_step
            slot = place_of(step)
            parts = [current[p] for p in range(share)]
            results = both_sides(parts, tables, which(step), True)
            for p in range(share):
                first, second = results[p]
                value = inner[step, p]
                real, imag = value[:, :width], value[:, width:]
                deposit(
                    slot, p, (real * first + imag * second, real * second - imag * first)
                )
                real, imag = window(slot, p)
                current[p] = jnp.concatenate(
                    [real * first + imag * second, real * second - imag * first], axis=1
                )
            return carry

        if kind != "B":
            lax.fori_loop(0, total, forward, 0)
        if kind == "T":
            for p in range(share):
                value = inner[total, p]
                first, second = value[:, :width], value[:, width:]
                misfit = first * first + second * second - wanted[p]
                loss = jnp.sum(misfit * misfit) / (width * width)
                loss_ref[p : p + 1, :] = jnp.full((1, 128), loss, jnp.float32)
                factor = 4.0 * misfit
                current[p] = jnp.concatenate([factor * first, factor * second], axis=1)
        if kind != "F":
            lax.fori_loop(0, total, backward, 0)

        copies.clear()
        if kind == "F":
            bring(inner.at[total], out_hbm)
            bring(inner, inner_hbm)
        else:
            bring(current, out_hbm)
            for j in range(group):
                section = core if j == 0 else 1 - core
                place = pl.ds(section * slots, slots)
                for b in range(blocks):
                    bring(store.at[place, :, b], grads[j].at[:, :, :, pl.ds(b * width, width)])
                bring(store.at[place, :, blocks], grads[group + j])
        for copy in copies:
            copy.wait()


def stage_call(kind, stage, cfg, operands, kept=()):
    group, slots, width, tile, share = cfg
    blocks = tile // width
    f32 = jnp.float32
    field = jax.ShapeDtypeStruct((share, width, 2 * width), f32)
    inner_shape = (group * slots + 1, share, width, 2 * width)
    grads = [jax.ShapeDtypeStruct((slots, 2, tile, tile), f32)] * group
    grads += [jax.ShapeDtypeStruct((slots, 2, tile, width), f32)] * group
    anywhere = pl.BlockSpec(memory_space=pl.ANY)
    scalars = pl.BlockSpec(memory_space=pltpu.SMEM)
    if kind == "F":
        outs = [field, jax.ShapeDtypeStruct(inner_shape, f32)]
    else:
        outs = [field] + grads
    out_specs = [anywhere] * len(outs)
    if kind == "T":
        outs.append(jax.ShapeDtypeStruct((share, 128), f32))
        out_specs.append(pl.BlockSpec(memory_space=pltpu.VMEM))
    aliases = {}
    for i in range(len(kept)):
        aliases[len(operands) + i] = 1 + i
    operands = list(operands) + list(kept)
    body = functools.partial(stage_kernel, kind, stage, cfg)
    if kind == "F" and kept:
        at = len(operands) - 1

        def body(*refs):
            stage_kernel(kind, stage, cfg, *refs[:at], *refs[at + 1 :])

    return pl.pallas_call(
        body,
        out_shape=outs,
        in_specs=[scalars] + [anywhere] * (len(operands) - 1),
        out_specs=out_specs,
        input_output_aliases=aliases,
        scratch_shapes=[
            pltpu.VMEM((group * slots, 2, blocks + 1, tile, width), f32),
            pltpu.VMEM((group * slots, 2, blocks + 1, tile, width), f32),
            pltpu.VMEM(inner_shape, f32),
            pltpu.VMEM((share, width, 2 * width), f32),
            pltpu.VMEM((2, 2, 2, 2 * width, 2 * width), jnp.bfloat16),
            pltpu.VMEM((share, width, width), f32),
            pltpu.SemaphoreType.DMA((8 + group * (blocks + 1),)),
        ],
        compiler_params=pltpu.CompilerParams(vmem_limit_bytes=48 * 1024 * 1024),
        name="stage_" + kind,
    )(*operands)


def shards(slices, section_counts, scan_rows, scan_columns, tick_order, measured, illumination):
    width = illumination.shape[-1]
    slots, _, tile, _ = slices.shape
    positions = scan_rows.shape[0]
    depth = lax.axis_size("depth")
    lat = lax.axis_size("lat")
    group = 2 if depth % 2 == 0 and positions % 2 == 0 else 1
    stages = depth // group
    share = positions // group
    cfg = (group, slots, width, tile, share)
    segment = lax.axis_index("depth")
    core = lax.rem(segment, group)
    stage = lax.div(segment, group)
    swap = [(d, d + 1 - 2 * (d % 2)) for d in range(depth)]

    def partner(block):
        return lax.ppermute(block, "depth", swap)

    def move(block, source, target):
        route = [(source * group + c, target * group + c) for c in range(group)]
        return lax.ppermute(block, "depth", route)

    rim = lax.ppermute(slices[..., :width], "lat", [((i + 1) % lat, i) for i in range(lat)])
    if group == 2:
        mains, rims = [slices, partner(slices)], [rim, partner(rim)]
        other = partner(section_counts)
        counts = jnp.where(
            core == 0,
            jnp.concatenate([section_counts, other]),
            jnp.concatenate([other, section_counts]),
        )
    else:
        mains, rims = [slices], [rim]
        counts = jnp.concatenate([section_counts, jnp.zeros_like(section_counts)])
    meta = jnp.concatenate(
        [
            jnp.stack([stage, core]),
            counts,
            lax.dynamic_slice_in_dim(scan_rows, core * share, share, 0),
            lax.dynamic_slice_in_dim(scan_columns, core * share, share, 0),
        ]
    ).astype(jnp.int32)
    tables = jnp.asarray(make_tables(width))
    launch = jnp.concatenate([illumination[0], illumination[1]], axis=1)
    field = jnp.broadcast_to(launch, (share, width, 2 * width))
    shared = (*mains, *rims)
    inner = ()
    for s in range(stages - 1):
        field, kept = stage_call("F", s, cfg, (meta, tables, field, *shared), inner)
        inner = (kept,)
        field = move(field, s, s + 1)
    last = stages - 1
    pull, *grads, loss = stage_call("T", last, cfg, (meta, tables, field, *shared, measured))
    losses = lax.all_gather(loss[:, 0], "depth", axis=0, tiled=True)[last * group * share :]
    for s in range(last - 1, -1, -1):
        pull = move(pull, s + 1, s)
        pull, *grads = stage_call(
            "B", s, cfg, (meta, tables, pull, *shared, inner[0]), tuple(grads)
        )
    main, over = grads[0], grads[group]
    if group == 2:
        over = over + partner(grads[group + 1])
        main = main + partner(grads[1])
    overflow = lax.ppermute(over, "lat", [(i, (i + 1) % lat) for i in range(lat)])
    slice_grad = main.at[..., :width].add(overflow)
    return (slice_grad, losses[tick_order[0]].reshape(1, positions))


def solution(mesh):
    placed = (
        P("depth", None, None, "lat"),
        P("depth"),
        P("lat"),
        P("lat"),
        P("lat", None),
        P("lat", None, None),
        P(),
    )
    return jax.shard_map(
        shards,
        mesh=mesh,
        in_specs=placed,
        out_specs=(P("depth", None, None, "lat"), P("lat", None)),
        check_vma=False,
    )
```

```python
import functools
import math

import jax
import jax.numpy as jnp
import ml_dtypes
import numpy as np
from jax import lax
from jax.experimental import pallas as pl
from jax.experimental.pallas import tpu as pltpu
from jax.sharding import PartitionSpec as P

fresnel = 12.0


def split_table(matrix):
    coarse = matrix.astype(ml_dtypes.bfloat16)
    fine = (matrix - coarse.astype(np.float64)).astype(ml_dtypes.bfloat16)
    return np.stack([coarse, fine])


def make_tables(width):
    index = np.arange(width)
    angle = 2.0 * math.pi / width * (index[:, None] * index[None, :] % width)
    dft = np.exp(-1j * angle) / math.sqrt(width)
    frequency = ((index + width // 2) % width - width // 2) / width
    spread = np.conj(dft) @ (np.exp(-1j * fresnel * frequency**2)[:, None] * dft)
    tables = []
    for matrix in (spread, dft):
        right = np.block([[matrix.real, matrix.imag], [-matrix.imag, matrix.real]])
        left = np.block([[matrix.real, -matrix.imag], [matrix.imag, matrix.real]])
        tables.append(np.stack([split_table(right), split_table(left)]))
    return np.stack(tables)


def halves(value):
    coarse = value.astype(jnp.bfloat16)
    fine = (value - coarse.astype(jnp.float32)).astype(jnp.bfloat16)
    return coarse, fine


def both_sides(parts, tables, which, adjoint):
    width = parts[0].shape[0]
    first, second = (1, 0) if adjoint else (0, 1)
    coarse, fine = halves(jnp.concatenate(parts, axis=0))
    high, low = tables[which, first, 0], tables[which, first, 1]
    half = jnp.dot(
        jnp.concatenate([coarse, fine, coarse], axis=1),
        jnp.concatenate([high, high, low], axis=0),
        preferred_element_type=jnp.float32,
    )
    rows = [half[p * width : (p + 1) * width] for p in range(len(parts))]
    turned = jnp.concatenate(
        [
            jnp.concatenate([r[:, :width] for r in rows], axis=1),
            jnp.concatenate([r[:, width:] for r in rows], axis=1),
        ],
        axis=0,
    )
    coarse, fine = halves(turned)
    high, low = tables[which, second, 0], tables[which, second, 1]
    full = jnp.dot(
        jnp.concatenate([high, high, low], axis=1),
        jnp.concatenate([coarse, fine, coarse], axis=0),
        preferred_element_type=jnp.float32,
    )
    return [
        (full[:width, p * width : (p + 1) * width], full[width:, p * width : (p + 1) * width])
        for p in range(len(parts))
    ]


def stage_kernel(kind, stage, batch, cfg, *refs):
    group, slots, width, tile, share, batches = cfg
    blocks = tile // width
    counts, (rows, columns, tables_hbm, entering_hbm), refs = (
        refs[:group],
        refs[group : group + 4],
        list(refs[group + 4 :]),
    )
    mains, rims = refs[:group], refs[group : 2 * group]
    refs = refs[2 * group :]
    if kind == "T":
        if batch:
            kept, refs = [refs[1 + i] for i in range(2 * group)], refs[:1] + refs[1 + 2 * group :]
        measured_hbm, out_hbm, loss_ref = refs[0], refs[1], refs[2 + 2 * group]
        grads = refs[2 : 2 + 2 * group]
        refs = refs[3 + 2 * group :]
    elif kind == "F":
        out_hbm, inner_hbm = refs[0], refs[1]
        refs = refs[2:]
    else:
        inner_hbm, kept = refs[0], refs[1 : 1 + 2 * group]
        out_hbm = refs[1 + 2 * group]
        grads = refs[2 + 2 * group : 2 + 4 * group]
        refs = refs[2 + 4 * group :]
    specimen, store, inner, current, tables, wanted, sems = refs

    segment = lax.axis_index("depth")
    core = lax.rem(segment, group)

    @pl.when(lax.div(segment, group) == stage)
    def _():
        base = (core * batches + batch) * share
        copies = []

        def bring(source, target):
            copy = pltpu.make_async_copy(source, target, sems.at[len(copies)])
            copy.start()
            copies.append(copy)

        bring(tables_hbm, tables)
        for j in range(group):
            section = core if j == 0 else 1 - core
            place = pl.ds(section * slots, slots)
            for b in range(blocks):
                bring(mains[j].at[:, :, :, pl.ds(b * width, width)], specimen.at[place, :, b])
            bring(rims[j], specimen.at[place, :, blocks])
        if kind == "B":
            bring(entering_hbm, current)
            bring(inner_hbm, inner)
        elif stage == 0:
            for p in range(share):
                for c in range(2):
                    bring(entering_hbm.at[c], inner.at[0, p, :, pl.ds(c * width, width)])
        else:
            bring(entering_hbm, inner.at[0])
        if kind == "T":
            bring(measured_hbm.at[pl.ds(base, share)], wanted)
        if kind != "F" and batch:
            for j in range(group):
                section = core if j == 0 else 1 - core
                place = pl.ds(section * slots, slots)
                for b in range(blocks):
                    bring(kept[j].at[:, :, :, pl.ds(b * width, width)], store.at[place, :, b])
                bring(kept[group + j], store.at[place, :, blocks])
        elif kind != "F":
            for slot in range(group * slots):
                store[slot] = jnp.zeros(store.shape[1:], jnp.float32)
        for copy in copies:
            copy.wait()

        count = counts[0][0]
        total = count
        if group == 2:
            total = counts[0][0] + counts[1][0]
            count = jnp.where(core == 0, counts[0][0], counts[1][0])
        lane = lax.broadcasted_iota(jnp.int32, (width, width), 1)

        def place_of(step):
            later = step >= count
            return jnp.where(later, slots + step - count, step)

        def corner(p):
            row, column = rows[base + p], columns[base + p]
            block = jnp.minimum(column // width, blocks - 1)
            return row, block, column - block * width

        def window(slot, p):
            row, block, shift = corner(p)
            back = lax.rem(width - shift, width)
            found = []
            for c in range(2):
                here = specimen[slot, c, block, pl.ds(row, width), :]
                after = specimen[slot, c, block + 1, pl.ds(row, width), :]
                found.append(pltpu.roll(jnp.where(lane >= shift, here, after), back, 1))
            return found

        def deposit(slot, p, pull):
            row, block, shift = corner(p)
            turn = lax.rem(shift, width)
            for c in range(2):
                turned = pltpu.roll(pull[c], turn, 1)
                here = jnp.where(lane >= shift, turned, 0.0)
                store[slot, c, block, pl.ds(row, width), :] += here
                store[slot, c, block + 1, pl.ds(row, width), :] += turned - here

        def which(step):
            return jnp.where(step == total - 1, 1, 0) if kind == "T" else 0

        def forward(step, carry):
            slot = place_of(step)
            parts = []
            for p in range(share):
                real, imag = window(slot, p)
                value = inner[step, p]
                first, second = value[:, :width], value[:, width:]
                parts.append(
                    jnp.concatenate(
                        [first * real - second * imag, first * imag + second * real], axis=1
                    )
                )
            results = both_sides(parts, tables, which(step), False)
            for p in range(share):
                inner[step + 1, p] = jnp.concatenate(results[p], axis=1)
            return carry

        def backward(back_step, carry):
            step = total - 1 - back_step
            slot = place_of(step)
            parts = [current[p] for p in range(share)]
            results = both_sides(parts, tables, which(step), True)
            for p in range(share):
                first, second = results[p]
                value = inner[step, p]
                real, imag = value[:, :width], value[:, width:]
                deposit(
                    slot, p, (real * first + imag * second, real * second - imag * first)
                )
                real, imag = window(slot, p)
                current[p] = jnp.concatenate(
                    [real * first + imag * second, real * second - imag * first], axis=1
                )
            return carry

        if kind != "B":
            lax.fori_loop(0, total, forward, 0)
        if kind == "T":
            for p in range(share):
                value = inner[total, p]
                first, second = value[:, :width], value[:, width:]
                misfit = first * first + second * second - wanted[p]
                loss = jnp.sum(misfit * misfit) / (width * width)
                loss_ref[p : p + 1, :] = jnp.full((1, 128), loss, jnp.float32)
                factor = 4.0 * misfit
                current[p] = jnp.concatenate([factor * first, factor * second], axis=1)
        if kind != "F":
            lax.fori_loop(0, total, backward, 0)

        copies.clear()
        if kind == "F":
            bring(inner.at[total], out_hbm)
            bring(inner, inner_hbm)
        else:
            bring(current, out_hbm)
            for j in range(group):
                section = core if j == 0 else 1 - core
                place = pl.ds(section * slots, slots)
                for b in range(blocks):
                    bring(store.at[place, :, b], grads[j].at[:, :, :, pl.ds(b * width, width)])
                bring(store.at[place, :, blocks], grads[group + j])
        for copy in copies:
            copy.wait()


def stage_call(kind, stage, batch, cfg, operands, kept=()):
    group, slots, width, tile, share, batches = cfg
    blocks = tile // width
    f32 = jnp.float32
    field = jax.ShapeDtypeStruct((share, width, 2 * width), f32)
    inner_shape = (group * slots + 1, share, width, 2 * width)
    grads = [jax.ShapeDtypeStruct((slots, 2, tile, tile), f32)] * group
    grads += [jax.ShapeDtypeStruct((slots, 2, tile, width), f32)] * group
    anywhere = pl.BlockSpec(memory_space=pl.ANY)
    scalars = pl.BlockSpec(memory_space=pltpu.SMEM)
    if kind == "F":
        outs = [field, jax.ShapeDtypeStruct(inner_shape, f32)]
    else:
        outs = [field] + grads
    out_specs = [anywhere] * len(outs)
    if kind == "T":
        outs.append(jax.ShapeDtypeStruct((share, 128), f32))
        out_specs.append(pl.BlockSpec(memory_space=pltpu.VMEM))
    aliases = {}
    for i in range(len(kept)):
        aliases[len(operands) + i] = 1 + i
    operands = list(operands) + list(kept)
    body = functools.partial(stage_kernel, kind, stage, batch, cfg)
    if kind == "F" and kept:
        at = len(operands) - 1

        def body(*refs):
            stage_kernel(kind, stage, batch, cfg, *refs[:at], *refs[at + 1 :])

    return pl.pallas_call(
        body,
        out_shape=outs,
        in_specs=[scalars] * (group + 2) + [anywhere] * (len(operands) - group - 2),
        out_specs=out_specs,
        input_output_aliases=aliases,
        scratch_shapes=[
            pltpu.VMEM((group * slots, 2, blocks + 1, tile, width), f32),
            pltpu.VMEM((group * slots, 2, blocks + 1, tile, width), f32),
            pltpu.VMEM(inner_shape, f32),
            pltpu.VMEM((share, width, 2 * width), f32),
            pltpu.VMEM((2, 2, 2, 2 * width, 2 * width), jnp.bfloat16),
            pltpu.VMEM((share, width, width), f32),
            pltpu.SemaphoreType.DMA((4 + 2 * share + 2 * group * (blocks + 1),)),
        ],
        compiler_params=pltpu.CompilerParams(vmem_limit_bytes=48 * 1024 * 1024),
        cost_estimate=pl.CostEstimate(
            flops=5_000_000_000, bytes_accessed=10_000_000, transcendentals=0
        ),
        name="stage_" + kind,
    )(*operands)


def shards(slices, section_counts, scan_rows, scan_columns, tick_order, measured, illumination):
    width = illumination.shape[-1]
    slots, _, tile, _ = slices.shape
    positions = scan_rows.shape[0]
    depth = lax.axis_size("depth")
    lat = lax.axis_size("lat")
    group = 2 if depth % 2 == 0 and positions % 2 == 0 else 1
    stages = depth // group
    batches = 2 if positions // group % 2 == 0 else 1
    share = positions // (group * batches)
    cfg = (group, slots, width, tile, share, batches)
    swap = [(d, d + 1 - 2 * (d % 2)) for d in range(depth)]

    def partner(block):
        return lax.ppermute(block, "depth", swap)

    def move(block, source, target):
        route = [(source * group + c, target * group + c) for c in range(group)]
        return lax.ppermute(block, "depth", route)

    rim = lax.ppermute(slices[..., :width], "lat", [((i + 1) % lat, i) for i in range(lat)])
    if group == 2:
        mains, rims = [slices, partner(slices)], [rim, partner(rim)]
        counts = [section_counts, partner(section_counts)]
    else:
        mains, rims, counts = [slices], [rim], [section_counts]
    tables = jnp.asarray(make_tables(width))
    scalars = (*counts, scan_rows, scan_columns, tables)
    shared = (*mains, *rims)
    every = range(batches)
    fields = [illumination] * batches
    inner = [()] * batches
    for s in range(stages - 1):
        for b in every:
            field, kept = stage_call("F", s, b, cfg, (*scalars, fields[b], *shared), inner[b])
            inner[b] = (kept,)
            fields[b] = move(field, s, s + 1)
    last = stages - 1
    pulls, losses, grads = [], [], ()
    for b in every:
        pull, *grads, loss = stage_call(
            "T", last, b, cfg, (*scalars, fields[b], *shared, measured), tuple(grads)
        )
        pulls.append(pull)
        losses.append(loss[:, 0])
    own = jnp.concatenate(losses)
    losses = lax.all_gather(own, "depth", axis=0, tiled=True)[last * positions :]
    for s in range(last - 1, -1, -1):
        for b in every:
            pulls[b], *grads = stage_call(
                "B",
                s,
                b,
                cfg,
                (*scalars, move(pulls[b], s + 1, s), *shared, *inner[b]),
                tuple(grads),
            )
    main, over = grads[0], grads[group]
    if group == 2:
        over = over + partner(grads[group + 1])
        main = main + partner(grads[1])
    overflow = lax.ppermute(over, "lat", [(i, (i + 1) % lat) for i in range(lat)])
    slice_grad = main.at[..., :width].add(overflow)
    return (slice_grad, losses[tick_order[0]].reshape(1, positions))


def solution(mesh):
    placed = (
        P("depth", None, None, "lat"),
        P("depth"),
        P("lat"),
        P("lat"),
        P("lat", None),
        P("lat", None, None),
        P(),
    )
    return jax.shard_map(
        shards,
        mesh=mesh,
        in_specs=placed,
        out_specs=(P("depth", None, None, "lat"), P("lat", None)),
        check_vma=False,
    )
```
